512 devices in a mesh: blk: 16 (over z), resp: 16 (over y_hi, x, core), head: 2 (over y_lo).
Axes of the slice: x: 4, y: 4 (y_hi: 2, y_lo: 2; y = y_hi * 2 + y_lo), z: 16, core: 2. Of those that a mesh axis runs over, the one named last changes fastest.
Arguments:
- queries: bfloat16 [65536, 4096], P(('blk', 'resp'), 'head'), may hold values from -6 to 6
- out_grad: bfloat16 [65536, 4096], P(('blk', 'resp'), 'head'), may hold values from -6 to 6
- prompt_keys: bfloat16 [2, 1024, 512], P(None, 'blk', 'head'), may hold values from -6 to 6
- prompt_values: bfloat16 [2, 1024, 512], P(None, 'blk', 'head'), may hold values from -6 to 6
- resp_prompt: int32 [256], P(('blk', 'resp')), may hold values from 0 to 1, as said below
- resp_len: int32 [256], P(('blk', 'resp')), may hold values from 128 to 256, as said below
Outputs:
- query_grad: bfloat16 [65536, 4096], P(('blk', 'resp'), 'head')
- prompt_key_grad: bfloat16 [2, 1024, 512], P(None, ('blk', 'resp'), 'head')
- prompt_value_grad: bfloat16 [2, 1024, 512], P(None, ('blk', 'resp'), 'head')
The draws below stay inside these ranges and needn't reach their ends.
Inputs may be any that keep to these rules, and one draw needn't show every extreme that they name: `resp_prompt`: each of the 2 prompts is named by exactly 128 responses. `resp_len`: multiples of 128; some response has 256 and some has 128.
All inputs are finite; a program needn't handle non-finite values.
Results may differ from the reference program's by a relative error of at most 0.019.
Values may be sent and summed in bfloat16 or wider, within the bound.
A program may use at most 128 MiB of HBM per device.

```python
import math
import jax
import jax.numpy as jnp
from jax import lax

QH = 32
KVH = 4
HD = 128
RLEN = 256
PROMPTS = 2
RESPONSES = 256
PLEN = 1024


def draw_queries(key, part):
    key = jax.random.fold_in(key, 1)
    shape_all = (RESPONSES * RLEN, QH * HD)
    base_draw = jnp.clip(jax.random.normal(key, shape_all, jnp.float32), -6.0, 6.0)
    return base_draw.astype(jnp.bfloat16)


def draw_prompt_keys(key, part):
    key = jax.random.fold_in(key, 2)
    shape_all = (PROMPTS, PLEN, KVH * HD)
    base_draw = jnp.clip(jax.random.normal(key, shape_all, jnp.float32), -6.0, 6.0)
    return base_draw.astype(jnp.bfloat16)


def draw_resp_prompt(key, part):
    key = jax.random.fold_in(key, 4)
    order_draw = jax.random.permutation(key, RESPONSES)
    return (order_draw % PROMPTS).astype(jnp.int32)


def draw_resp_len(key, part):
    key = jax.random.fold_in(key, 3)
    block_count = jax.random.randint(key, (RESPONSES,), 1, RLEN // 128 + 1)
    block_count = block_count.at[0].set(RLEN // 128).at[1].set(1)
    return (block_count * 128).astype(jnp.int32)


def block_scale(stream_key, dims, pieces, low, top_value):
    factor_of = 1.0
    for axis_at, blocks in pieces:
        heights = jax.random.uniform(jax.random.fold_in(jax.random.fold_in(stream_key, 6), axis_at), (blocks,), jnp.float32, low / len(pieces), top_value / len(pieces))
        factor_of = factor_of * jnp.repeat(jnp.exp(heights), dims[axis_at] // blocks).reshape((-1,) + (1,) * (len(dims) - 1 - axis_at))
    return factor_of


def bell_draw(stream_key, shape, deviation, bound, pieces=(), kind=jnp.bfloat16):
    factor_of = block_scale(stream_key, shape, pieces, -0.22, 0.18) if pieces else 1.0
    result = jax.random.normal(stream_key, shape, jnp.float32) * deviation * factor_of
    return jnp.minimum(jnp.maximum(result, -bound), bound).astype(kind)


def setup_inputs(seed: int = 0) -> dict:
    arg_keys = jax.random.split(jax.random.key(seed), 7)
    queries = draw_queries(jax.random.fold_in(arg_keys[6], 71), 0)
    out_grad = bell_draw(arg_keys[1], (RESPONSES * RLEN, QH * HD), 1.0, 6.0, ((0, 256), (1, 2)))
    prompt_keys = draw_prompt_keys(jax.random.fold_in(arg_keys[6], 71), 0)
    prompt_values = bell_draw(arg_keys[3], (PROMPTS, PLEN, KVH * HD), 1.0, 6.0, ((1, 16), (2, 2)))
    resp_prompt = draw_resp_prompt(jax.random.fold_in(arg_keys[6], 71), 0)
    resp_len = draw_resp_len(jax.random.fold_in(arg_keys[6], 71), 0)
    return {"queries": queries, "out_grad": out_grad, "prompt_keys": prompt_keys, "prompt_values": prompt_values, "resp_prompt": resp_prompt, "resp_len": resp_len}


def one_response(query_row, grad_row, key_block, value_block, length):
    scaling = 1.0 / math.sqrt(HD)
    group_size = QH // KVH
    live_rows = jnp.arange(RLEN, dtype=jnp.int32) < length
    query_full = query_row.astype(jnp.float32).reshape(RLEN, KVH, group_size, HD)
    grad_full = jnp.where(live_rows[:, None], grad_row.astype(jnp.float32), jnp.float32(0.0))
    grad_full = grad_full.reshape(RLEN, KVH, group_size, HD)
    key_full = key_block.astype(jnp.float32).reshape(PLEN, KVH, HD)
    value_full = value_block.astype(jnp.float32).reshape(PLEN, KVH, HD)
    scores = jnp.einsum('rkgd,pkd->kgrp', query_full, key_full) * scaling
    row_peak = lax.optimization_barrier(jnp.max(scores, axis=-1, keepdims=True))
    exp_scores = jnp.exp(scores - row_peak)
    probs = exp_scores / lax.optimization_barrier(jnp.sum(exp_scores, axis=-1, keepdims=True))
    dprob = jnp.einsum('rkgd,pkd->kgrp', grad_full, value_full)
    row_delta = lax.optimization_barrier(jnp.sum(probs * dprob, axis=-1, keepdims=True))
    dscore = probs * (dprob - row_delta)
    weights = lax.optimization_barrier(probs.astype(jnp.bfloat16)).astype(jnp.float32)
    dscore_low = lax.optimization_barrier(dscore.astype(jnp.bfloat16)).astype(jnp.float32)
    query_part = jnp.einsum('kgrp,pkd->rkgd', dscore_low, key_full) * scaling
    key_part = jnp.einsum('kgrp,rkgd->pkd', dscore_low, query_full) * scaling
    value_part = jnp.einsum('kgrp,rkgd->pkd', weights, grad_full)
    query_part = jnp.where(live_rows[:, None], query_part.reshape(RLEN, QH * HD), jnp.float32(0.0))
    return (query_part.astype(jnp.bfloat16), key_part.reshape(PLEN, KVH * HD), value_part.reshape(PLEN, KVH * HD))

def reference(queries, out_grad, prompt_keys, prompt_values, resp_prompt, resp_len):
    query_all = queries.reshape(RESPONSES, RLEN, QH * HD)
    grad_all = out_grad.reshape(RESPONSES, RLEN, QH * HD)

    def cycle_step(carry_state, item_tuple):
        key_sum, value_sum = carry_state
        query_row, grad_row, prompt, length = item_tuple
        key_block = lax.dynamic_index_in_dim(prompt_keys, prompt, 0, keepdims=False)
        value_block = lax.dynamic_index_in_dim(prompt_values, prompt, 0, keepdims=False)
        query_part, key_part, value_part = one_response(query_row, grad_row, key_block, value_block, length)
        chosen = (jnp.arange(PROMPTS, dtype=jnp.int32) == prompt).astype(jnp.float32)[:, None, None]
        return ((key_sum + chosen * key_part[None], value_sum + chosen * value_part[None]), query_part)
    initial = (jnp.zeros((PROMPTS, PLEN, KVH * HD), jnp.float32), jnp.zeros((PROMPTS, PLEN, KVH * HD), jnp.float32))
    (key_sum, value_sum), query_parts = lax.scan(cycle_step, initial, (query_all, grad_all, resp_prompt, resp_len))
    return (query_parts.reshape(RESPONSES * RLEN, QH * HD), key_sum.astype(jnp.bfloat16), value_sum.astype(jnp.bfloat16))
```

```python
import functools
import math

import jax
import jax.numpy as jnp
from jax import lax
from jax.experimental import pallas as pl
from jax.experimental.pallas import tpu as pltpu
from jax.sharding import PartitionSpec as P

HD = 128
MESH = pl.DeviceIdType.MESH
F32 = jnp.float32
BF16 = jnp.bfloat16
NX = 4
NY = 2
CT = 8
JUMP = 2


def gather_plan(blocks):
    up, down = blocks // 2, (blocks - 1) // 2
    steps, slots, gone = [], {0: 0}, 0
    while True:
        sends = [(-gone, d, -gone - d) for d in range(1, JUMP + 1) if gone + d <= up]
        sends += [(gone, -d, gone + d) for d in range(1, JUMP + 1) if gone + d <= down]
        if not sends:
            return steps, slots
        for _, _, offset in sends:
            slots[offset] = len(slots)
        steps.append(sends)
        gone += JUMP


def kernel(
    blocks,
    groups,
    q_hbm,
    g_hbm,
    k_in,
    v_in,
    prompt_ref,
    len_ref,
    dq_hbm,
    dk_out,
    dv_out,
    q_ref,
    g_ref,
    dq_ref,
    kv,
    kc,
    acc,
    core_out,
    core_in,
    x_out,
    x_in,
    x_own,
    y_out,
    y_in,
    z_out,
    z_in,
    last_out,
    last_in,
    flag,
    in_sem,
    out_sem,
    kv_send,
    kv_recv,
    share_send,
    share_recv,
    core_send,
    core_recv,
    x_send,
    x_recv,
    y_send,
    y_recv,
    z_send,
    z_recv,
    last_send,
    last_recv,
    flag_send,
    flag_recv,
):
    b, s = lax.axis_index("blk"), lax.axis_index("resp")
    y, x, c = s // (2 * NX), (s // 2) % NX, s % 2
    other_core = {"resp": s + 1 - 2 * c}
    other_y = {"resp": s + (1 - 2 * y) * (2 * NX)}
    steps, slots = gather_plan(blocks)

    def at_x(i):
        return {"resp": y * (2 * NX) + ((x + i) % NX) * 2 + c}

    def at_blk(offset):
        return {"blk": (b + offset + blocks) % blocks}

    def remote(src, dst, send, recv, to):
        return pltpu.make_async_remote_copy(
            src_ref=src, dst_ref=dst, send_sem=send, recv_sem=recv, device_id=to, device_id_type=MESH
        )

    load_q = pltpu.make_async_copy(q_hbm, q_ref, in_sem.at[0])
    load_g = pltpu.make_async_copy(g_hbm, g_ref, in_sem.at[1])
    load_q.start()
    load_g.start()

    partners = [other_core, other_y] + [at_x(i) for i in range(1, NX)]
    partners += [at_blk(o) for o in slots if o != 0]
    barrier = pltpu.get_barrier_semaphore()
    for to in partners:
        pl.semaphore_signal(barrier, inc=1, device_id=to, device_id_type=MESH)

    for kind, ref in enumerate((k_in, v_in)):
        for p in range(2):
            rows = ref[p].astype(F32)
            parts = [
                rows[(iy * NX + ix) * CT : (iy * NX + ix + 1) * CT]
                for ix in range(NX)
                for iy in range(NY)
            ]
            rows = jnp.concatenate(parts, axis=0).astype(BF16)
            for h in range(2):
                kv[kind, h, 0, p] = rows[:, h * HD : (h + 1) * HD]
    mine = prompt_ref[0].astype(F32)
    flag[0] = jnp.full((16, HD), 1.0, F32).astype(BF16) * mine.astype(BF16)
    pl.semaphore_wait(barrier, len(partners))

    flag_copy = remote(flag.at[0], flag.at[1], flag_send, flag_recv, other_core)
    flag_copy.start()

    def block_copy(h, step, i):
        held, jump, offset = steps[step][i]
        return remote(
            kv.at[c, h, slots[held]],
            kv.at[c, h, slots[offset]],
            kv_send.at[h, slots[offset]],
            kv_recv.at[h, slots[offset]],
            at_blk(jump),
        )

    def share_copy(h, step):
        first, count = slots[steps[step][0][2]], len(steps[step])
        part = kv.at[c, h, pl.ds(first, count)]
        return remote(part, part, share_send.at[h, step], share_recv.at[h, step], other_core)

    def gather_begin(h):
        for i in range(len(steps[0])):
            block_copy(h, 0, i).start()

    def gather_step(h, step):
        onward = set()
        if step + 1 < len(steps):
            onward = {held for held, _, _ in steps[step + 1]}
        for wanted in (True, False):
            for i, (_, _, offset) in enumerate(steps[step]):
                if (offset in onward) == wanted:
                    block_copy(h, step, i).wait_recv()
            if wanted and step + 1 < len(steps):
                for i in range(len(steps[step + 1])):
                    block_copy(h, step + 1, i).start()
        share_copy(h, step).start()

    def gather_end(h):
        for step in range(len(steps)):
            share_copy(h, step).wait_recv()

    gather_begin(0)
    gather_begin(1)
    for step in range(len(steps)):
        gather_step(0, step)
    gather_end(0)
    load_q.wait()
    load_g.wait()
    flag_copy.wait_recv()

    scaling = 1.0 / math.sqrt(HD)
    rate = scaling * math.log2(math.e)
    length = len_ref[0]
    rows_live = lax.broadcasted_iota(jnp.int32, (q_ref.shape[0], HD), 0) < length

    def dot(a, o, ca, co):
        return lax.dot_general(a, o, (((ca,), (co,)), ((), ())), preferred_element_type=F32)

    def begin_head(h):
        second = prompt_ref[0] == 1
        for kind in range(2):
            block = jnp.where(second, kv[kind, h, :, 1], kv[kind, h, :, 0])
            kc[kind] = block.reshape(kc.shape[1], HD)
        acc[h] = jnp.zeros_like(acc[h])

    def unit(u):
        cols = pl.ds(pl.multiple_of(u * HD, HD), HD)
        q = q_ref[:, cols]
        g = jnp.where(rows_live, g_ref[:, cols], jnp.zeros((), BF16))
        scores = dot(kc[0], q, 1, 1)
        dprob = dot(kc[1], g, 1, 1)
        top = jnp.max(scores, axis=0, keepdims=True)
        e = jnp.exp2((scores - top) * rate)
        total = jnp.sum(e, axis=0, keepdims=True)
        probs = e * (1.0 / total)
        delta = jnp.sum(probs * dprob, axis=0, keepdims=True)
        dscore = (probs * (dprob - delta)).astype(BF16)
        weights = probs.astype(BF16)
        h = u // groups
        acc[h, 0] += dot(dscore, q, 1, 0).reshape(acc.shape[2:])
        acc[h, 1] += dot(weights, g, 1, 0).reshape(acc.shape[2:])
        dq_ref[:, cols] = (dot(dscore, kc[0], 0, 0) * scaling).astype(BF16)

    def core_copy(h):
        return remote(core_out.at[h], core_in.at[h], core_send.at[h], core_recv.at[h], other_core)

    def x_copy(h, i):
        return remote(
            x_out.at[h, i], x_in.at[h, i], x_send.at[h, i], x_recv.at[h, i], at_x(i + 1)
        )

    def y_copy(h):
        return remote(y_out.at[h], y_in.at[h], y_send.at[h], y_recv.at[h], other_y)

    def z_copy(h, offset):
        at = slots[offset]
        return remote(
            z_out.at[h, at], z_in.at[h, at], z_send.at[h, at], z_recv.at[h, at], at_blk(offset)
        )

    def reduce_core(h):
        core_out[h] = (acc[h, 1 - c] * jnp.where(c == 0, 1.0, scaling)).astype(BF16)
        core_copy(h).start()

    def reduce_x(h):
        core_copy(h).wait_recv()
        theirs = flag[1, 0:1].astype(F32)
        own = [1.0 - mine, mine]
        other = [1.0 - theirs, theirs]
        factor = jnp.where(c == 0, scaling, 1.0)

        def chunk(at):
            a = acc[h, c, :, at] * factor
            o = core_in[h, :, at].astype(F32)
            both = [a * own[p] + o * other[p] for p in range(2)]
            return [
                jnp.concatenate([t[:, iy * CT : (iy + 1) * CT] for t in both], axis=1)
                for iy in range(NY)
            ]

        for i in range(1, NX):
            for iy, part in enumerate(chunk((x + i) % NX)):
                x_out[h, i - 1, iy] = part.astype(BF16)
            x_copy(h, i - 1).start()
        for iy, part in enumerate(chunk(x)):
            x_own[h, iy] = part

    def reduce_y(h):
        for i in range(NX - 1):
            x_copy(h, i).wait_recv()

        def total(at):
            t = x_own[h, at]
            for i in range(NX - 1):
                t += x_in[h, i, at].astype(F32)
            return t

        y_out[h] = total(1 - y).astype(BF16)
        y_copy(h).start()
        x_own[h, 0] = total(y)

    def reduce_z(h):
        y_copy(h).wait_recv()
        t = x_own[h, 0] + y_in[h].astype(F32)
        x_own[h, 0] = t
        z_out[h] = t.astype(BF16)
        for offset in slots:
            if offset != 0:
                z_copy(h, offset).start()

    def reduce_last(h):
        for offset in slots:
            if offset != 0:
                z_copy(h, offset).wait_recv()
        t = x_own[h, 0, 0]
        for at in range(1, blocks):
            t += z_in[h, at].astype(F32)
        last_out[h] = t.astype(BF16)

    def body(u, carry):
        @pl.when(u == groups)
        def _():
            gather_end(1)

        @pl.when(u % groups == 0)
        def _():
            begin_head(u // groups)

        unit(u)
        for step in range(len(steps)):

            @pl.when(u == step + 1)
            def _(step=step):
                gather_step(1, step)

        phases = (reduce_core, reduce_x, reduce_y, reduce_z, reduce_last)
        for n, phase in enumerate(phases):

            @pl.when(u == groups - 1 + min(2 * n, groups))
            def _(phase=phase):
                phase(0)

        return carry

    lax.fori_loop(0, 2 * groups, body, 0)
    store_q = pltpu.make_async_copy(dq_ref, dq_hbm, out_sem)
    store_q.start()
    reduce_core(1)
    reduce_x(1)
    reduce_y(1)
    reduce_z(1)
    reduce_last(1)

    final = remote(last_out, last_in, last_send, last_recv, other_core)
    final.start()
    final.wait_recv()
    half = CT // 2
    for kind, out in enumerate((dk_out, dv_out)):
        for h in range(2):
            tile = jnp.where(c == kind, last_out[h].astype(F32), last_in[h].astype(F32))
            for p in range(2):
                low = tile[p * CT : p * CT + half]
                high = tile[p * CT + half : (p + 1) * CT]
                out[p, :, h * HD : (h + 1) * HD] = jnp.where(c == 0, low, high).astype(BF16)

    flag_copy.wait_send()
    for h in range(2):
        for step in range(len(steps)):
            for i in range(len(steps[step])):
                block_copy(h, step, i).wait_send()
        for step in range(len(steps)):
            share_copy(h, step).wait_send()
        core_copy(h).wait_send()
        for i in range(NX - 1):
            x_copy(h, i).wait_send()
        y_copy(h).wait_send()
        for offset in slots:
            if offset != 0:
                z_copy(h, offset).wait_send()
    final.wait_send()
    store_q.wait()


def solution(mesh):
    blocks = mesh.shape["blk"]

    def shards(queries, out_grad, prompt_keys, prompt_values, resp_prompt, resp_len):
        rows, columns = queries.shape
        block_rows = prompt_keys.shape[1]
        groups = columns // HD // 2
        steps = len(gather_plan(blocks)[0])
        dma = pltpu.SemaphoreType.DMA
        return pl.pallas_call(
            functools.partial(kernel, blocks, groups),
            out_shape=(
                jax.ShapeDtypeStruct(queries.shape, BF16),
                jax.ShapeDtypeStruct((2, CT // 2, 2 * HD), BF16),
                jax.ShapeDtypeStruct((2, CT // 2, 2 * HD), BF16),
            ),
            in_specs=[
                pl.BlockSpec(memory_space=pl.ANY),
                pl.BlockSpec(memory_space=pl.ANY),
                pl.BlockSpec(memory_space=pltpu.VMEM),
                pl.BlockSpec(memory_space=pltpu.VMEM),
                pl.BlockSpec(memory_space=pltpu.SMEM),
                pl.BlockSpec(memory_space=pltpu.SMEM),
            ],
            out_specs=(
                pl.BlockSpec(memory_space=pl.ANY),
                pl.BlockSpec(memory_space=pltpu.VMEM),
                pl.BlockSpec(memory_space=pltpu.VMEM),
            ),
            scratch_shapes=[
                pltpu.VMEM((rows, columns), BF16),
                pltpu.VMEM((rows, columns), BF16),
                pltpu.VMEM((rows, columns), BF16),
                pltpu.VMEM((2, 2, blocks, 2, block_rows, HD), BF16),
                pltpu.VMEM((2, blocks * block_rows, HD), BF16),
                pltpu.VMEM((2, 2, blocks, NX, NY * CT, HD), F32),
                pltpu.VMEM((2, blocks, NX, NY * CT, HD), BF16),
                pltpu.VMEM((2, blocks, NX, NY * CT, HD), BF16),
                pltpu.VMEM((2, NX - 1, NY, blocks, 2 * CT, HD), BF16),
                pltpu.VMEM((2, NX - 1, NY, blocks, 2 * CT, HD), BF16),
                pltpu.VMEM((2, NY, blocks, 2 * CT, HD), F32),
                pltpu.VMEM((2, blocks, 2 * CT, HD), BF16),
                pltpu.VMEM((2, blocks, 2 * CT, HD), BF16),
                pltpu.VMEM((2, blocks, 2 * CT, HD), BF16),
                pltpu.VMEM((2, blocks, 2 * CT, HD), BF16),
                pltpu.VMEM((2, 2 * CT, HD), BF16),
                pltpu.VMEM((2, 2 * CT, HD), BF16),
                pltpu.VMEM((2, 16, HD), BF16),
                dma((2,)),
                dma,
                dma((2, blocks)),
                dma((2, blocks)),
                dma((2, steps)),
                dma((2, steps)),
                dma((2,)),
                dma((2,)),
                dma((2, NX - 1)),
                dma((2, NX - 1)),
                dma((2,)),
                dma((2,)),
                dma((2, blocks)),
                dma((2, blocks)),
                dma,
                dma,
                dma,
                dma,
            ],
            compiler_params=pltpu.CompilerParams(
                collective_id=0, has_side_effects=True, vmem_limit_bytes=56 << 20
            ),
        )(queries, out_grad, prompt_keys, prompt_values, resp_prompt, resp_len)

    rows = P(("blk", "resp"), "head")
    blocks_in = P(None, "blk", "head")
    each = P(("blk", "resp"))
    sums = P(None, ("blk", "resp"), "head")
    return jax.shard_map(
        shards,
        mesh=mesh,
        in_specs=(rows, rows, blocks_in, blocks_in, each, each),
        out_specs=(rows, sums, sums),
        check_vma=False,
    )
```

```python
import functools
import math

import jax
import jax.numpy as jnp
from jax import lax
from jax.experimental import pallas as pl
from jax.experimental.pallas import tpu as pltpu
from jax.sharding import PartitionSpec as P

HD = 128
MESH = pl.DeviceIdType.MESH
F32 = jnp.float32
BF16 = jnp.bfloat16
NX = 4
NY = 2
PLANE = NX * NY
CT = 8
TILE = NY * CT
UNITS = 2


def kernel(
    blocks,
    groups,
    q_hbm,
    g_hbm,
    k_hbm,
    v_hbm,
    prompt_hbm,
    len_hbm,
    dq_ref,
    dk_out,
    dv_out,
    k_in,
    v_in,
    q_ref,
    g_ref,
    prompt_ref,
    len_ref,
    order,
    kv,
    kc,
    acc,
    core_out,
    core_in,
    plane_out,
    plane_in,
    z_out,
    z_in,
    z_own,
    last_out,
    last_in,
    flag,
    in_sem,
    kvz_send,
    kvz_recv,
    kvp_send,
    kvp_recv,
    kvc_send,
    kvc_recv,
    core_send,
    core_recv,
    plane_send,
    plane_recv,
    z_send,
    z_recv,
    last_send,
    last_recv,
    flag_send,
    flag_recv,
):
    b, s = lax.axis_index("blk"), lax.axis_index("resp")
    y, x, c = s // (2 * NX), (s // 2) % NX, s % 2
    other_core = {"resp": s + 1 - 2 * c}

    def shifted(i):
        return (y + i) % NY, (x + i // NY) % NX

    def behind(i):
        return (y + i) % NY, (x + NX - i // NY) % NX

    def at_plane(i):
        py, px = shifted(i)
        return {"resp": (py * NX + px) * 2 + c}

    def at_blk(offset):
        return {"blk": (b + offset) % blocks}

    def remote(src, dst, send, recv, to):
        return pltpu.make_async_remote_copy(
            src_ref=src, dst_ref=dst, send_sem=send, recv_sem=recv, device_id=to, device_id_type=MESH
        )

    others = range(1, blocks)
    mates = range(1, PLANE)
    partners = [other_core] + [at_plane(i) for i in mates] + [at_blk(o) for o in others]
    barrier = pltpu.get_barrier_semaphore()
    for to in partners:
        pl.semaphore_signal(barrier, inc=1, device_id=to, device_id_type=MESH)

    loads = [
        pltpu.make_async_copy(k_hbm, k_in, in_sem.at[0]),
        pltpu.make_async_copy(v_hbm, v_in, in_sem.at[1]),
        pltpu.make_async_copy(prompt_hbm, prompt_ref, in_sem.at[2]),
        pltpu.make_async_copy(len_hbm, len_ref, in_sem.at[3]),
        pltpu.make_async_copy(q_hbm, q_ref, in_sem.at[4]),
        pltpu.make_async_copy(g_hbm, g_ref, in_sem.at[5]),
    ]
    for load in loads:
        load.start()

    loads[0].wait()
    loads[1].wait()
    rows = jnp.where(c == 0, k_in[y].astype(F32), v_in[y].astype(F32))
    for ix in range(NX):
        parts = [rows[(iy * NX + ix) * CT : (iy * NX + ix + 1) * CT] for iy in range(NY)]
        order[ix] = jnp.concatenate(parts, axis=0)
    tile = order[x].astype(BF16)
    for h in range(2):
        kv[c, h, y, x, 0] = tile[:, h * HD : (h + 1) * HD]
    loads[2].wait()
    mine = prompt_ref[0].astype(F32)
    flag[0] = jnp.full((16, HD), 1.0, F32).astype(BF16) * mine.astype(BF16)
    pl.semaphore_wait(barrier, len(partners))

    def kvz_copy(h, offset):
        sent = kv.at[c, h, y, x, 0]
        return remote(
            sent, kv.at[c, h, y, x, blocks - offset], kvz_send.at[h, offset], kvz_recv.at[h, offset], at_blk(offset)
        )

    def kvp_copy(h, i, wait=False):
        py, px = behind(i) if wait else (y, x)
        part = kv.at[c, h, py, px]
        return remote(kv.at[c, h, y, x], part, kvp_send.at[h, i], kvp_recv.at[h, i], at_plane(i))

    def kvc_copy(h):
        return remote(kv.at[c, h], kv.at[c, h], kvc_send.at[h], kvc_recv.at[h], other_core)

    def gather_blk(h):
        for offset in others:
            kvz_copy(h, offset).start()

    def gather_plane(h):
        for offset in others:
            kvz_copy(h, offset).wait_recv()
        for i in mates:
            kvp_copy(h, i).start()

    def gather_core(h):
        for i in mates:
            kvp_copy(h, i, True).wait_recv()
        kvc_copy(h).start()

    flag_copy = remote(flag.at[0], flag.at[1], flag_send, flag_recv, other_core)
    flag_copy.start()
    gather_blk(0)
    gather_blk(1)
    gather_plane(0)
    gather_plane(1)
    gather_core(0)
    for load in loads[3:]:
        load.wait()
    flag_copy.wait_recv()
    kvc_copy(0).wait_recv()

    scaling = 1.0 / math.sqrt(HD)
    rate = scaling * math.log2(math.e)
    rows_live = lax.broadcasted_iota(jnp.int32, (q_ref.shape[0], HD), 0) < len_ref[0]

    def dot(a, o, ca, co):
        return lax.dot_general(a, o, (((ca,), (co,)), ((), ())), preferred_element_type=F32)

    def begin_head(h):
        second = prompt_ref[0] == 1
        for kind in range(2):
            kc[kind] = jnp.where(second, kv[kind, h, 1], kv[kind, h, 0])
        acc[h] = jnp.zeros_like(acc[h])

    positions = NX * blocks * TILE

    def units(t):
        keys, values = kc[0].reshape(positions, HD), kc[1].reshape(positions, HD)
        h = t // (groups // UNITS)
        started = []
        for i in range(UNITS):
            cols = pl.ds(pl.multiple_of((t * UNITS + i) * HD, HD), HD)
            q = q_ref[:, cols]
            g = jnp.where(rows_live, g_ref[:, cols], jnp.zeros((), BF16))
            started.append((cols, q, g, dot(keys, q, 1, 1), dot(values, g, 1, 1)))
        key_sum = value_sum = 0.0
        for cols, q, g, scores, dprob in started:
            top = jnp.max(scores, axis=0, keepdims=True)
            e = jnp.exp2((scores - top) * rate)
            probs = e * (1.0 / jnp.sum(e, axis=0, keepdims=True))
            delta = jnp.sum(probs * dprob, axis=0, keepdims=True)
            dscore = (probs * (dprob - delta)).astype(BF16)
            weights = probs.astype(BF16)
            key_sum += dot(dscore, q, 1, 0)
            value_sum += dot(weights, g, 1, 0)
            dq_ref[:, cols] = (dot(dscore, keys, 0, 0) * scaling).astype(BF16)
        acc[h, 0] += key_sum.reshape(acc.shape[2:])
        acc[h, 1] += value_sum.reshape(acc.shape[2:])

    def core_copy(h):
        return remote(core_out.at[h], core_in.at[h], core_send.at[h], core_recv.at[h], other_core)

    def plane_copy(h, i):
        return remote(
            plane_out.at[h, i], plane_in.at[h, i], plane_send.at[h, i], plane_recv.at[h, i], at_plane(i)
        )

    def z_copy(h, at):
        return remote(z_out.at[h, at], z_in.at[h, at], z_send.at[h, at], z_recv.at[h, at], at_blk(at))

    def reduce_core(h):
        core_out[h] = (acc[h, 1 - c] * jnp.where(c == 0, 1.0, scaling)).astype(BF16)
        core_copy(h).start()

    def reduce_plane(h):
        core_copy(h).wait_recv()
        theirs = flag[1, 0:1].astype(F32)
        own = [1.0 - mine, mine]
        other = [1.0 - theirs, theirs]
        factor = jnp.where(c == 0, scaling, 1.0)
        for dx in (2, 1, 3, 0):
            at = (x + dx) % NX
            a = acc[h, c, at] * factor
            o = core_in[h, at].astype(F32)
            both = [a * own[p] + o * other[p] for p in range(2)]
            for iy in range(NY):
                part = jnp.concatenate([t[:, iy * CT : (iy + 1) * CT] for t in both], axis=1)
                plane_out[h, dx * NY + (iy + NY - y) % NY] = part.astype(BF16)
            for i in range(dx * NY, dx * NY + NY):
                if i:
                    plane_copy(h, i).start()

    def reduce_z(h):
        for i in mates:
            plane_copy(h, i).wait_recv()
        total = plane_out[h, 0].astype(F32)
        for i in mates:
            total += plane_in[h, i].astype(F32)
        z_out[h] = total.astype(BF16)
        z_own[h] = total[0]
        for at in others:
            z_copy(h, at).start()

    def reduce_last(h):
        for at in others:
            z_copy(h, at).wait_recv()
        total = z_own[h]
        for at in others:
            total += z_in[h, at].astype(F32)
        last_out[h] = total.astype(BF16)

    turns = groups // UNITS

    def body(t, carry):
        @pl.when(t == 0)
        def _():
            begin_head(0)

        @pl.when(t == turns)
        def _():
            kvc_copy(1).wait_recv()
            begin_head(1)

        units(t)

        @pl.when(t == turns - 2)
        def _():
            gather_core(1)

        @pl.when(t == turns - 1)
        def _():
            reduce_core(0)

        @pl.when(t == turns)
        def _():
            reduce_plane(0)

        return carry

    lax.fori_loop(0, 2 * turns, body, 0)
    reduce_core(1)
    reduce_z(0)
    reduce_plane(1)
    reduce_last(0)
    reduce_z(1)
    reduce_last(1)

    final = remote(last_out, last_in, last_send, last_recv, other_core)
    final.start()
    final.wait_recv()
    half = CT // 2
    for kind, out in enumerate((dk_out, dv_out)):
        for h in range(2):
            tile = jnp.where(c == kind, last_out[h].astype(F32), last_in[h].astype(F32))
            for p in range(2):
                low = tile[p * CT : p * CT + half]
                high = tile[p * CT + half : (p + 1) * CT]
                out[p, :, h * HD : (h + 1) * HD] = jnp.where(c == 0, low, high).astype(BF16)

    flag_copy.wait_send()
    for h in range(2):
        for offset in others:
            kvz_copy(h, offset).wait_send()
            z_copy(h, offset).wait_send()
        for i in mates:
            kvp_copy(h, i).wait_send()
            plane_copy(h, i).wait_send()
        kvc_copy(h).wait_send()
        core_copy(h).wait_send()
    final.wait_send()


def solution(mesh):
    blocks = mesh.shape["blk"]

    def shards(queries, out_grad, prompt_keys, prompt_values, resp_prompt, resp_len):
        rows, columns = queries.shape
        groups = columns // HD // 2
        dma = pltpu.SemaphoreType.DMA
        vmem, smem = pltpu.VMEM, pltpu.SMEM
        in_hbm = pl.BlockSpec(memory_space=pltpu.HBM)
        in_vmem = pl.BlockSpec(memory_space=pltpu.VMEM)
        return pl.pallas_call(
            functools.partial(kernel, blocks, groups),
            out_shape=(
                vmem(queries.shape, BF16),
                vmem((2, CT // 2, 2 * HD), BF16),
                vmem((2, CT // 2, 2 * HD), BF16),
            ),
            in_specs=[in_hbm] * 6,
            out_specs=(in_vmem, in_vmem, in_vmem),
            scratch_shapes=[
                vmem(prompt_keys.shape, BF16),
                vmem(prompt_values.shape, BF16),
                vmem((rows, columns), BF16),
                vmem((rows, columns), BF16),
                smem((1,), jnp.int32),
                smem((1,), jnp.int32),
                vmem((NX, TILE, 2 * HD), F32),
                vmem((2, 2, 2, NX, blocks, TILE, HD), BF16),
                vmem((2, NX, blocks, TILE, HD), BF16),
                vmem((2, 2, NX, blocks, TILE, HD), F32),
                vmem((2, NX, blocks, TILE, HD), BF16),
                vmem((2, NX, blocks, TILE, HD), BF16),
                vmem((2, PLANE, blocks, 2 * CT, HD), BF16),
                vmem((2, PLANE, blocks, 2 * CT, HD), BF16),
                vmem((2, blocks, 2 * CT, HD), BF16),
                vmem((2, blocks, 2 * CT, HD), BF16),
                vmem((2, 2 * CT, HD), F32),
                vmem((2, 2 * CT, HD), BF16),
                vmem((2, 2 * CT, HD), BF16),
                vmem((2, 16, HD), BF16),
                dma((6,)),
                dma((2, blocks)),
                dma((2, blocks)),
                dma((2, PLANE)),
                dma((2, PLANE)),
                dma((2,)),
                dma((2,)),
                dma((2,)),
                dma((2,)),
                dma((2, PLANE)),
                dma((2, PLANE)),
                dma((2, blocks)),
                dma((2, blocks)),
                dma,
                dma,
                dma,
                dma,
            ],
            compiler_params=pltpu.CompilerParams(
                collective_id=0, has_side_effects=True, vmem_limit_bytes=56 << 20
            ),
        )(queries, out_grad, prompt_keys, prompt_values, resp_prompt, resp_len)

    rows = P(("blk", "resp"), "head")
    blocks_in = P(None, "blk", "head")
    each = P(("blk", "resp"))
    sums = P(None, ("blk", "resp"), "head")
    return jax.shard_map(
        shards,
        mesh=mesh,
        in_specs=(rows, rows, blocks_in, blocks_in, each, each),
        out_specs=(rows, sums, sums),
        check_vma=False,
    )
```

```python
import functools
import math

import jax
import jax.numpy as jnp
from jax import lax
from jax.experimental import pallas as pl
from jax.experimental.pallas import tpu as pltpu
from jax.sharding import PartitionSpec as P

HD = 128
MESH = pl.DeviceIdType.MESH
F32 = jnp.float32
BF16 = jnp.bfloat16
NX = 4
NY = 2
PLANE = NX * NY
CT = 8
TILE = NY * CT
NEAR = 4
UNITS = 4


def kernel(
    blocks,
    groups,
    q_hbm,
    g_hbm,
    k_hbm,
    v_hbm,
    prompt_hbm,
    len_hbm,
    dq_ref,
    dk_out,
    dv_out,
    k_in,
    v_in,
    q_ref,
    g_ref,
    prompt_ref,
    len_ref,
    order,
    kv,
    kc,
    qg,
    terms,
    acc,
    core_out,
    core_in,
    plane_out,
    plane_in,
    z_out,
    z_in,
    z_own,
    last_out,
    last_in,
    flag,
    in_sem,
    kvz_send,
    kvz_recv,
    kvp_send,
    kvp_recv,
    kvc_send,
    kvc_recv,
    core_send,
    core_recv,
    plane_send,
    plane_recv,
    z_send,
    z_recv,
    last_send,
    last_recv,
    flag_send,
    flag_recv,
):
    rows = q_ref.shape[0]
    b, s = lax.axis_index("blk"), lax.axis_index("resp")
    y, x, c = s // (2 * NX), (s // 2) % NX, s % 2
    other_core = {"resp": s + 1 - 2 * c}

    def shifted(i):
        return (y + i) % NY, (x + i // NY) % NX

    def behind(i):
        return (y + i) % NY, (x + NX - i // NY) % NX

    def at_plane(i):
        py, px = shifted(i)
        return {"resp": (py * NX + px) * 2 + c}

    def at_blk(offset):
        return {"blk": (b + offset) % blocks}

    def remote(src, dst, send, recv, to):
        return pltpu.make_async_remote_copy(
            src_ref=src, dst_ref=dst, send_sem=send, recv_sem=recv, device_id=to, device_id_type=MESH
        )

    def each(indices, act):
        def step(i, carry):
            act(i)
            return carry

        lax.fori_loop(indices.start, indices.stop, step, 0)

    others = range(1, blocks)
    mates = range(1, PLANE)
    partners = [other_core] + [at_plane(i) for i in mates] + [at_blk(o) for o in others]
    barrier = pltpu.get_barrier_semaphore()
    for to in partners:
        pl.semaphore_signal(barrier, inc=1, device_id=to, device_id_type=MESH)

    loads = [
        pltpu.make_async_copy(k_hbm, k_in, in_sem.at[0]),
        pltpu.make_async_copy(v_hbm, v_in, in_sem.at[1]),
        pltpu.make_async_copy(prompt_hbm, prompt_ref, in_sem.at[2]),
        pltpu.make_async_copy(len_hbm, len_ref, in_sem.at[3]),
        pltpu.make_async_copy(q_hbm, q_ref, in_sem.at[4]),
        pltpu.make_async_copy(g_hbm, g_ref, in_sem.at[5]),
    ]
    for load in loads:
        load.start()

    loads[0].wait()
    loads[1].wait()
    block = jnp.where(c == 0, k_in[y].astype(F32), v_in[y].astype(F32))
    for ix in range(NX):
        parts = [block[(iy * NX + ix) * CT : (iy * NX + ix + 1) * CT] for iy in range(NY)]
        order[ix] = jnp.concatenate(parts, axis=0)
    tile = order[x].astype(BF16)
    for h in range(2):
        kv[c, h, y, x, NEAR] = tile[:, h * HD : (h + 1) * HD]
    loads[2].wait()
    mine = prompt_ref[0].astype(F32)
    flag[0] = jnp.full((16, HD), 1.0, F32).astype(BF16) * mine.astype(BF16)
    pl.semaphore_wait(barrier, len(partners))

    near = range(0, 2 * NEAR + 1)
    far = range(2 * NEAR + 1, blocks)
    halves = (near, far)

    def kvz_copy(h, offset):
        return remote(
            kv.at[c, h, y, x, NEAR],
            kv.at[c, h, y, x, (blocks + NEAR - offset) % blocks],
            kvz_send.at[h, offset],
            kvz_recv.at[h, offset],
            at_blk(offset),
        )

    def each_offset(half, act):
        if half is far:
            each(range(NEAR + 1, blocks - NEAR), act)
        else:
            each(range(1, NEAR + 1), act)
            each(range(blocks - NEAR, blocks), act)

    def part_of(half):
        return pl.ds(half.start, len(half))

    def kvp_copy(h, half, i, wait=False):
        py, px = behind(i) if wait else (y, x)
        part, n = part_of(half), halves.index(half)
        return remote(
            kv.at[c, h, y, x, part],
            kv.at[c, h, py, px, part],
            kvp_send.at[h, n, i],
            kvp_recv.at[h, n, i],
            at_plane(i),
        )

    def kvc_copy(h, half, i, kind):
        py, px = behind(i)
        part, n = kv.at[kind, h, py, px, part_of(half)], halves.index(half)
        return remote(part, part, kvc_send.at[h, n, i], kvc_recv.at[h, n, i], other_core)

    def gather_blk(h):
        for half in halves:
            each_offset(half, lambda offset: kvz_copy(h, offset).start())

    def gather_plane(h):
        for half in halves:
            each_offset(half, lambda offset: kvz_copy(h, offset).wait_recv())
            each(mates, lambda i: kvp_copy(h, half, i).start())
            kvc_copy(h, half, 0, c).start()

    def gather_core(h):
        for half in halves:

            def passed(i):
                kvp_copy(h, half, i, True).wait_recv()
                kvc_copy(h, half, i, c).start()

            each(mates, passed)

    def gather_end(h):
        for half in halves:
            each(range(PLANE), lambda i: kvc_copy(h, half, i, 1 - c).wait_recv())

    flag_copy = remote(flag.at[0], flag.at[1], flag_send, flag_recv, other_core)
    flag_copy.start()
    gather_blk(0)
    for load in loads[3:]:
        load.wait()
    rows_live = lax.broadcasted_iota(jnp.int32, (rows, HD), 0) < len_ref[0]

    def place(u, carry):
        h, at = u // groups, pl.ds(pl.multiple_of(u % groups * rows, rows), rows)
        cols = pl.ds(pl.multiple_of(u * HD, HD), HD)
        qg[h, 0, at] = q_ref[:, cols]
        qg[h, 1, at] = jnp.where(rows_live, g_ref[:, cols], jnp.zeros((), BF16))
        return carry

    lax.fori_loop(0, 2 * groups, place, 0)
    gather_plane(0)
    gather_blk(1)
    gather_core(0)
    gather_plane(1)
    flag_copy.wait_recv()
    gather_end(0)

    scaling = 1.0 / math.sqrt(HD)
    rate = scaling * math.log2(math.e)
    def dot(a, o, ca, co):
        return lax.dot_general(a, o, (((ca,), (co,)), ((), ())), preferred_element_type=F32)

    positions = NX * blocks * TILE

    def choose(h):
        second = prompt_ref[0] == 1
        for kind in range(2):
            kc[h, kind] = jnp.where(second, kv[kind, h, 1], kv[kind, h, 0])

    def softmax_units(h):
        def step(t, carry):
            keys, values = kc[h, 0].reshape(positions, HD), kc[h, 1].reshape(positions, HD)
            started = []
            for i in range(UNITS):
                at = pl.ds(pl.multiple_of((t * UNITS + i) * rows, rows), rows)
                scores = dot(keys, qg[h, 0, at], 1, 1)
                started.append((at, scores, dot(values, qg[h, 1, at], 1, 1)))
            for at, scores, dprob in started:
                top = jnp.max(scores, axis=0, keepdims=True)
                e = jnp.exp2((scores - top) * rate)
                probs = e * (1.0 / jnp.sum(e, axis=0, keepdims=True))
                delta = jnp.sum(probs * dprob, axis=0, keepdims=True)
                dscore = (probs * (dprob - delta)).astype(BF16)
                terms[h, 0, :, :, at] = dscore.reshape(NX, blocks * TILE, rows)
                terms[h, 1, :, :, at] = probs.astype(BF16).reshape(NX, blocks * TILE, rows)
            return carry

        lax.fori_loop(0, groups // UNITS, step, 0)

    def query_units(h):
        def step(t, carry):
            keys = kc[h, 0].reshape(positions, HD)
            for i in range(UNITS):
                u = t * UNITS + i
                at = pl.ds(pl.multiple_of(u * rows, rows), rows)
                cols = pl.ds(pl.multiple_of((h * groups + u) * HD, HD), HD)
                dscore = terms[h, 0, :, :, at].reshape(positions, rows)
                dq_ref[:, cols] = (dot(dscore, keys, 0, 0) * scaling).astype(BF16)
            return carry

        lax.fori_loop(0, groups // UNITS, step, 0)

    def chunk_at(n):
        return (x + NX - 1 - n) % NX

    def core_copy(h, n):
        at = chunk_at(n)
        return remote(
            core_out.at[h, at], core_in.at[h, at], core_send.at[h, n], core_recv.at[h, n], other_core
        )

    def plane_copy(h, half, i):
        part, n = part_of(half), halves.index(half)
        return remote(
            plane_out.at[h, i, part],
            plane_in.at[h, i, part],
            plane_send.at[h, n, i],
            plane_recv.at[h, n, i],
            at_plane(i),
        )

    def z_copy(h, at):
        return remote(z_out.at[h, at], z_in.at[h, at], z_send.at[h, at], z_recv.at[h, at], at_blk(at + blocks - NEAR))

    def reduce_chunk(h, n):
        at = chunk_at(n)
        out = dot(terms[h, 1 - c, at], qg[h, 1 - c], 1, 0) * jnp.where(c == 0, 1.0, scaling)
        core_out[h, at] = out.astype(BF16).reshape(core_out.shape[2:])
        core_copy(h, n).start()
        own = dot(terms[h, c, at], qg[h, c], 1, 0) * jnp.where(c == 0, scaling, 1.0)
        acc[h, at] = own.reshape(acc.shape[2:])

    def reduce_plane(h, n):
        core_copy(h, n).wait_recv()
        theirs = flag[1, 0:1].astype(F32)
        own = [1.0 - mine, mine]
        other = [1.0 - theirs, theirs]
        dx, at = NX - 1 - n, chunk_at(n)
        a, o = acc[h, at], core_in[h, at].astype(F32)
        both = [a * own[p] + o * other[p] for p in range(2)]
        for iy in range(NY):
            part = jnp.concatenate([t[:, iy * CT : (iy + 1) * CT] for t in both], axis=1)
            plane_out[h, dx * NY + (iy + NY - y) % NY] = part.astype(BF16)
        plane_copy(h, far, dx * NY + 1).start()

        @pl.when(dx > 0)
        def _():
            plane_copy(h, far, dx * NY).start()

    def reduce_begin(h):
        def step(n):
            @pl.when(n < NX)
            def _():
                reduce_chunk(h, n)

            @pl.when(n > 0)
            def _():
                reduce_plane(h, n - 1)

        each(range(NX + 1), step)
        each(mates, lambda i: plane_copy(h, near, i).start())

    def each_other(half, act):
        if half is far:
            each(far, act)
        else:
            each(range(NEAR), act)
            each(range(NEAR + 1, 2 * NEAR + 1), act)

    def reduce_z(h):
        for half in (far, near):
            part = part_of(half)
            z_own[h, part] = plane_out[h, 0, part].astype(F32)

            def arrived(i):
                plane_copy(h, half, i).wait_recv()
                z_own[h, part] += plane_in[h, i, part].astype(F32)

            each(mates, arrived)
            z_out[h, part] = z_own[h, part].astype(BF16)
            each_other(half, lambda at: z_copy(h, at).start())

    def reduce_last(h):
        def arrived(at):
            z_copy(h, at).wait_recv()
            z_own[h, NEAR] += z_in[h, at].astype(F32)

        each_other(near, arrived)
        each_other(far, arrived)
        last_out[h] = z_own[h, NEAR].astype(BF16)

    def first_half(h):
        @pl.when(h == 1)
        def _():
            gather_core(1)
            gather_end(1)

        choose(h)
        softmax_units(h)
        reduce_begin(h)

    def second_half(h):
        reduce_z(h)
        query_units(h)

    each(range(2), first_half)
    each(range(2), second_half)
    def drain(h):
        each(others, lambda offset: kvz_copy(h, offset).wait_send())
        for half in halves:
            each_other(half, lambda at: z_copy(h, at).wait_send())

            def over_plane(i):
                kvp_copy(h, half, i).wait_send()
                plane_copy(h, half, i).wait_send()

            each(mates, over_plane)
            each(range(PLANE), lambda i: kvc_copy(h, half, i, c).wait_send())
        each(range(NX), lambda n: core_copy(h, n).wait_send())

    each(range(2), drain)
    flag_copy.wait_send()
    each(range(2), reduce_last)

    final = remote(last_out, last_in, last_send, last_recv, other_core)
    final.start()
    final.wait_recv()
    half = CT // 2
    for kind, out in enumerate((dk_out, dv_out)):
        for h in range(2):
            tile = jnp.where(c == kind, last_out[h].astype(F32), last_in[h].astype(F32))
            for p in range(2):
                low = tile[p * CT : p * CT + half]
                high = tile[p * CT + half : (p + 1) * CT]
                out[p, :, h * HD : (h + 1) * HD] = jnp.where(c == 0, low, high).astype(BF16)

    final.wait_send()


def solution(mesh):
    blocks = mesh.shape["blk"]

    def shards(queries, out_grad, prompt_keys, prompt_values, resp_prompt, resp_len):
        rows, columns = queries.shape
        groups = columns // HD // 2
        dma = pltpu.SemaphoreType.DMA
        vmem, smem = pltpu.VMEM, pltpu.SMEM
        in_hbm = pl.BlockSpec(memory_space=pltpu.HBM)
        in_vmem = pl.BlockSpec(memory_space=pltpu.VMEM)
        return pl.pallas_call(
            functools.partial(kernel, blocks, groups),
            out_shape=(
                vmem(queries.shape, BF16),
                vmem((2, CT // 2, 2 * HD), BF16),
                vmem((2, CT // 2, 2 * HD), BF16),
            ),
            in_specs=[in_hbm] * 6,
            out_specs=(in_vmem, in_vmem, in_vmem),
            scratch_shapes=[
                vmem(prompt_keys.shape, BF16),
                vmem(prompt_values.shape, BF16),
                vmem((rows, columns), BF16),
                vmem((rows, columns), BF16),
                smem((1,), jnp.int32),
                smem((1,), jnp.int32),
                vmem((NX, TILE, 2 * HD), F32),
                vmem((2, 2, 2, NX, blocks, TILE, HD), BF16),
                vmem((2, 2, NX, blocks, TILE, HD), BF16),
                vmem((2, 2, groups * rows, HD), BF16),
                vmem((2, 2, NX, blocks * TILE, groups * rows), BF16),
                vmem((2, NX, blocks, TILE, HD), F32),
                vmem((2, NX, blocks, TILE, HD), BF16),
                vmem((2, NX, blocks, TILE, HD), BF16),
                vmem((2, PLANE, blocks, 2 * CT, HD), BF16),
                vmem((2, PLANE, blocks, 2 * CT, HD), BF16),
                vmem((2, blocks, 2 * CT, HD), BF16),
                vmem((2, blocks, 2 * CT, HD), BF16),
                vmem((2, blocks, 2 * CT, HD), F32),
                vmem((2, 2 * CT, HD), BF16),
                vmem((2, 2 * CT, HD), BF16),
                vmem((2, 16, HD), BF16),
                dma((6,)),
                dma((2, blocks)),
                dma((2, blocks)),
                dma((2, 2, PLANE)),
                dma((2, 2, PLANE)),
                dma((2, 2, PLANE)),
                dma((2, 2, PLANE)),
                dma((2, NX)),
                dma((2, NX)),
                dma((2, 2, PLANE)),
                dma((2, 2, PLANE)),
                dma((2, blocks)),
                dma((2, blocks)),
                dma,
                dma,
                dma,
                dma,
            ],
            compiler_params=pltpu.CompilerParams(
                collective_id=0, has_side_effects=True, vmem_limit_bytes=56 << 20
            ),
        )(queries, out_grad, prompt_keys, prompt_values, resp_prompt, resp_len)

    rows = P(("blk", "resp"), "head")
    blocks_in = P(None, "blk", "head")
    each = P(("blk", "resp"))
    sums = P(None, ("blk", "resp"), "head")
    return jax.shard_map(
        shards,
        mesh=mesh,
        in_specs=(rows, rows, blocks_in, blocks_in, each, each),
        out_specs=(rows, sums, sums),
        check_vma=False,
    )
```

```python
import functools
import math

import jax
import jax.numpy as jnp
from jax import lax
from jax.experimental import pallas as pl
from jax.experimental.pallas import tpu as pltpu
from jax.sharding import PartitionSpec as P

HD = 128
MESH = pl.DeviceIdType.MESH
F32 = jnp.float32
BF16 = jnp.bfloat16
NX = 4
NY = 2
PLANE = NX * NY
CT = 8
TILE = NY * CT
NEAR = 4
UNITS = 8
QUERY_UNITS = 4


def kernel(
    blocks,
    groups,
    q_hbm,
    g_hbm,
    k_hbm,
    v_hbm,
    prompt_hbm,
    len_hbm,
    dq_ref,
    dk_out,
    dv_out,
    k_in,
    v_in,
    q_ref,
    g_ref,
    prompt_ref,
    len_ref,
    order,
    kv,
    kc,
    qg,
    terms,
    acc,
    core_out,
    core_in,
    plane_out,
    plane_in,
    z_out,
    z_in,
    z_own,
    last_out,
    last_in,
    flag,
    in_sem,
    kvz_send,
    kvz_recv,
    kvp_send,
    kvp_recv,
    kvc_send,
    kvc_recv,
    core_send,
    core_recv,
    plane_send,
    plane_recv,
    z_send,
    z_recv,
    last_send,
    last_recv,
    flag_send,
    flag_recv,
):
    rows = q_ref.shape[0]
    b, s = lax.axis_index("blk"), lax.axis_index("resp")
    y, x, c = s // (2 * NX), (s // 2) % NX, s % 2
    other_core = {"resp": s + 1 - 2 * c}

    def shifted(i):
        return (y + i) % NY, (x + i // NY) % NX

    def behind(i):
        return (y + i) % NY, (x + NX - i // NY) % NX

    def at_plane(i):
        py, px = shifted(i)
        return {"resp": (py * NX + px) * 2 + c}

    def at_blk(offset):
        return {"blk": (b + offset) % blocks}

    def remote(src, dst, send, recv, to):
        return pltpu.make_async_remote_copy(
            src_ref=src, dst_ref=dst, send_sem=send, recv_sem=recv, device_id=to, device_id_type=MESH
        )

    def each(indices, act):
        def step(i, carry):
            act(i)
            return carry

        lax.fori_loop(indices.start, indices.stop, step, 0)

    others = range(1, blocks)
    mates = range(1, PLANE)
    partners = [other_core] + [at_plane(i) for i in mates] + [at_blk(o) for o in others]
    barrier = pltpu.get_barrier_semaphore()
    for to in partners:
        pl.semaphore_signal(barrier, inc=1, device_id=to, device_id_type=MESH)

    loads = [
        pltpu.make_async_copy(k_hbm, k_in, in_sem.at[0]),
        pltpu.make_async_copy(v_hbm, v_in, in_sem.at[1]),
        pltpu.make_async_copy(prompt_hbm, prompt_ref, in_sem.at[2]),
        pltpu.make_async_copy(len_hbm, len_ref, in_sem.at[3]),
        pltpu.make_async_copy(q_hbm, q_ref, in_sem.at[4]),
        pltpu.make_async_copy(g_hbm, g_ref, in_sem.at[5]),
    ]
    for load in loads:
        load.start()

    loads[0].wait()
    loads[1].wait()
    block = jnp.where(c == 0, k_in[y].astype(F32), v_in[y].astype(F32))
    for ix in range(NX):
        parts = [block[(iy * NX + ix) * CT : (iy * NX + ix + 1) * CT] for iy in range(NY)]
        order[ix] = jnp.concatenate(parts, axis=0)
    tile = order[x].astype(BF16)
    for h in range(2):
        kv[c, h, y, x, NEAR] = tile[:, h * HD : (h + 1) * HD]
    loads[2].wait()
    mine = prompt_ref[0].astype(F32)
    flag[0] = jnp.full((16, HD), 1.0, F32).astype(BF16) * mine.astype(BF16)
    pl.semaphore_wait(barrier, len(partners))

    near = range(0, 2 * NEAR + 1)
    far = range(2 * NEAR + 1, blocks)
    halves = (near, far)

    def kvz_copy(h, offset):
        return remote(
            kv.at[c, h, y, x, NEAR],
            kv.at[c, h, y, x, (blocks + NEAR - offset) % blocks],
            kvz_send.at[h, offset],
            kvz_recv.at[h, offset],
            at_blk(offset),
        )

    def each_offset(half, act):
        if half is far:
            each(range(NEAR + 1, blocks - NEAR), act)
        else:
            each(range(1, NEAR + 1), act)
            each(range(blocks - NEAR, blocks), act)

    def part_of(half):
        return pl.ds(half.start, len(half))

    def kvp_copy(h, half, i, wait=False):
        py, px = behind(i) if wait else (y, x)
        part, n = part_of(half), halves.index(half)
        return remote(
            kv.at[c, h, y, x, part],
            kv.at[c, h, py, px, part],
            kvp_send.at[h, n, i],
            kvp_recv.at[h, n, i],
            at_plane(i),
        )

    def kvc_copy(h, half, i, kind):
        py, px = behind(i)
        part, n = kv.at[kind, h, py, px, part_of(half)], halves.index(half)
        return remote(part, part, kvc_send.at[h, n, i], kvc_recv.at[h, n, i], other_core)

    def gather_blk(h):
        for half in halves:
            each_offset(half, lambda offset: kvz_copy(h, offset).start())

    def gather_plane(h):
        for half in halves:
            each_offset(half, lambda offset: kvz_copy(h, offset).wait_recv())
            each(mates, lambda i: kvp_copy(h, half, i).start())
            kvc_copy(h, half, 0, c).start()

    def gather_core(h):
        for half in halves:

            def passed(i):
                kvp_copy(h, half, i, True).wait_recv()
                kvc_copy(h, half, i, c).start()

            each(mates, passed)

    def gather_end(h):
        for half in halves:
            each(range(PLANE), lambda i: kvc_copy(h, half, i, 1 - c).wait_recv())

    flag_copy = remote(flag.at[0], flag.at[1], flag_send, flag_recv, other_core)
    flag_copy.start()
    gather_blk(0)
    for load in loads[3:]:
        load.wait()
    rows_live = lax.broadcasted_iota(jnp.int32, (rows, HD), 0) < len_ref[0]

    def place(u, carry):
        h, at = u // groups, pl.ds(pl.multiple_of(u % groups * rows, rows), rows)
        cols = pl.ds(pl.multiple_of(u * HD, HD), HD)
        qg[h, 0, at] = q_ref[:, cols]
        qg[h, 1, at] = jnp.where(rows_live, g_ref[:, cols], jnp.zeros((), BF16))
        return carry

    lax.fori_loop(0, 2 * groups, place, 0)
    gather_plane(0)
    gather_blk(1)
    gather_core(0)
    gather_plane(1)
    flag_copy.wait_recv()
    gather_end(0)

    scaling = 1.0 / math.sqrt(HD)
    rate = scaling * math.log2(math.e)
    def dot(a, o, ca, co):
        return lax.dot_general(a, o, (((ca,), (co,)), ((), ())), preferred_element_type=F32)

    positions = NX * blocks * TILE

    def choose(h):
        second = prompt_ref[0] == 1
        for kind in range(2):
            kc[h, kind] = jnp.where(second, kv[kind, h, 1], kv[kind, h, 0])

    def softmax_units(h):
        def step(t, carry):
            keys, values = kc[h, 0].reshape(positions, HD), kc[h, 1].reshape(positions, HD)
            started = []
            for i in range(UNITS):
                at = pl.ds(pl.multiple_of((t * UNITS + i) * rows, rows), rows)
                scores = dot(keys, qg[h, 0, at], 1, 1)
                started.append((at, scores, dot(values, qg[h, 1, at], 1, 1)))
            for at, scores, dprob in started:
                top = jnp.max(scores, axis=0, keepdims=True)
                e = jnp.exp2((scores - top) * rate)
                probs = e * (1.0 / jnp.sum(e, axis=0, keepdims=True))
                delta = jnp.sum(probs * dprob, axis=0, keepdims=True)
                dscore = (probs * (dprob - delta)).astype(BF16)
                terms[h, 0, :, :, at] = dscore.reshape(NX, blocks * TILE, rows)
                terms[h, 1, :, :, at] = probs.astype(BF16).reshape(NX, blocks * TILE, rows)
            return carry

        lax.fori_loop(0, groups // UNITS, step, 0)

    def query_units(h):
        def step(t, carry):
            keys = kc[h, 0].reshape(positions, HD)
            for i in range(QUERY_UNITS):
                u = t * QUERY_UNITS + i
                at = pl.ds(pl.multiple_of(u * rows, rows), rows)
                cols = pl.ds(pl.multiple_of((h * groups + u) * HD, HD), HD)
                dscore = terms[h, 0, :, :, at].reshape(positions, rows)
                dq_ref[:, cols] = (dot(dscore, keys, 0, 0) * scaling).astype(BF16)
            return carry

        lax.fori_loop(0, groups // QUERY_UNITS, step, 0)

    def chunk_at(n):
        return (x + NX - 1 - n) % NX

    def core_copy(h, n):
        at = chunk_at(n)
        return remote(
            core_out.at[h, at], core_in.at[h, at], core_send.at[h, n], core_recv.at[h, n], other_core
        )

    def plane_copy(h, half, i):
        part, n = part_of(half), halves.index(half)
        return remote(
            plane_out.at[h, i, part],
            plane_in.at[h, i, part],
            plane_send.at[h, n, i],
            plane_recv.at[h, n, i],
            at_plane(i),
        )

    def z_copy(h, at):
        return remote(z_out.at[h, at], z_in.at[h, at], z_send.at[h, at], z_recv.at[h, at], at_blk(at + blocks - NEAR))

    def reduce_chunk(h, n):
        at = chunk_at(n)
        out = dot(terms[h, 1 - c, at], qg[h, 1 - c], 1, 0) * jnp.where(c == 0, 1.0, scaling)
        core_out[h, at] = out.astype(BF16).reshape(core_out.shape[2:])
        core_copy(h, n).start()
        own = dot(terms[h, c, at], qg[h, c], 1, 0) * jnp.where(c == 0, scaling, 1.0)
        acc[h, at] = own.reshape(acc.shape[2:])

    def reduce_plane(h, n):
        core_copy(h, n).wait_recv()
        theirs = flag[1, 0:1].astype(F32)
        own = [1.0 - mine, mine]
        other = [1.0 - theirs, theirs]
        dx, at = NX - 1 - n, chunk_at(n)
        a, o = acc[h, at], core_in[h, at].astype(F32)
        both = [a * own[p] + o * other[p] for p in range(2)]
        for iy in range(NY):
            part = jnp.concatenate([t[:, iy * CT : (iy + 1) * CT] for t in both], axis=1)
            plane_out[h, dx * NY + (iy + NY - y) % NY] = part.astype(BF16)
        plane_copy(h, far, dx * NY + 1).start()

        @pl.when(dx > 0)
        def _():
            plane_copy(h, far, dx * NY).start()

    def reduce_begin(h):
        def step(n):
            @pl.when(n < NX)
            def _():
                reduce_chunk(h, n)

            @pl.when(n > 0)
            def _():
                reduce_plane(h, n - 1)

        each(range(NX + 1), step)
        each(mates, lambda i: plane_copy(h, near, i).start())

    def each_other(half, act):
        if half is far:
            each(far, act)
        else:
            each(range(NEAR), act)
            each(range(NEAR + 1, 2 * NEAR + 1), act)

    def reduce_z(h):
        for half in (far, near):
            part = part_of(half)
            z_own[h, part] = plane_out[h, 0, part].astype(F32)

            def arrived(i):
                plane_copy(h, half, i).wait_recv()
                z_own[h, part] += plane_in[h, i, part].astype(F32)

            each(mates, arrived)
            z_out[h, part] = z_own[h, part].astype(BF16)
            each_other(half, lambda at: z_copy(h, at).start())

    def reduce_last(h):
        def arrived(at):
            z_copy(h, at).wait_recv()
            z_own[h, NEAR] += z_in[h, at].astype(F32)

        each_other(near, arrived)
        each_other(far, arrived)
        last_out[h] = z_own[h, NEAR].astype(BF16)

    def first_half(h):
        @pl.when(h == 1)
        def _():
            gather_core(1)
            gather_end(1)

        choose(h)
        softmax_units(h)
        reduce_begin(h)

    def second_half(h):
        reduce_z(h)
        query_units(h)

    each(range(2), first_half)
    each(range(2), second_half)
    def drain(h):
        each(others, lambda offset: kvz_copy(h, offset).wait_send())
        for half in halves:
            each_other(half, lambda at: z_copy(h, at).wait_send())

            def over_plane(i):
                kvp_copy(h, half, i).wait_send()
                plane_copy(h, half, i).wait_send()

            each(mates, over_plane)
            each(range(PLANE), lambda i: kvc_copy(h, half, i, c).wait_send())
        each(range(NX), lambda n: core_copy(h, n).wait_send())

    each(range(2), drain)
    flag_copy.wait_send()
    each(range(2), reduce_last)

    final = remote(last_out, last_in, last_send, last_recv, other_core)
    final.start()
    final.wait_recv()
    half = CT // 2
    for kind, out in enumerate((dk_out, dv_out)):
        for h in range(2):
            tile = jnp.where(c == kind, last_out[h].astype(F32), last_in[h].astype(F32))
            for p in range(2):
                low = tile[p * CT : p * CT + half]
                high = tile[p * CT + half : (p + 1) * CT]
                out[p, :, h * HD : (h + 1) * HD] = jnp.where(c == 0, low, high).astype(BF16)

    final.wait_send()


def store_kernel(dq_ref, dk_ref, dv_ref, dq_hbm, dk_hbm, dv_hbm, sem):
    pairs = ((dq_ref, dq_hbm), (dk_ref, dk_hbm), (dv_ref, dv_hbm))
    copies = [pltpu.make_async_copy(src, dst, sem.at[n]) for n, (src, dst) in enumerate(pairs)]
    for copy in copies:
        copy.start()
    for copy in copies:
        copy.wait()


def solution(mesh):
    blocks = mesh.shape["blk"]

    def shards(queries, out_grad, prompt_keys, prompt_values, resp_prompt, resp_len):
        rows, columns = queries.shape
        groups = columns // HD // 2
        dma = pltpu.SemaphoreType.DMA
        vmem, smem = pltpu.VMEM, pltpu.SMEM
        in_hbm = pl.BlockSpec(memory_space=pltpu.HBM)
        in_vmem = pl.BlockSpec(memory_space=pltpu.VMEM)
        grads = pl.pallas_call(
            functools.partial(kernel, blocks, groups),
            out_shape=(
                vmem(queries.shape, BF16),
                vmem((2, CT // 2, 2 * HD), BF16),
                vmem((2, CT // 2, 2 * HD), BF16),
            ),
            in_specs=[in_hbm] * 6,
            out_specs=(in_vmem, in_vmem, in_vmem),
            scratch_shapes=[
                vmem(prompt_keys.shape, BF16),
                vmem(prompt_values.shape, BF16),
                vmem((rows, columns), BF16),
                vmem((rows, columns), BF16),
                smem((1,), jnp.int32),
                smem((1,), jnp.int32),
                vmem((NX, TILE, 2 * HD), F32),
                vmem((2, 2, 2, NX, blocks, TILE, HD), BF16),
                vmem((2, 2, NX, blocks, TILE, HD), BF16),
                vmem((2, 2, groups * rows, HD), BF16),
                vmem((2, 2, NX, blocks * TILE, groups * rows), BF16),
                vmem((2, NX, blocks, TILE, HD), F32),
                vmem((2, NX, blocks, TILE, HD), BF16),
                vmem((2, NX, blocks, TILE, HD), BF16),
                vmem((2, PLANE, blocks, 2 * CT, HD), BF16),
                vmem((2, PLANE, blocks, 2 * CT, HD), BF16),
                vmem((2, blocks, 2 * CT, HD), BF16),
                vmem((2, blocks, 2 * CT, HD), BF16),
                vmem((2, blocks, 2 * CT, HD), F32),
                vmem((2, 2 * CT, HD), BF16),
                vmem((2, 2 * CT, HD), BF16),
                vmem((2, 16, HD), BF16),
                dma((6,)),
                dma((2, blocks)),
                dma((2, blocks)),
                dma((2, 2, PLANE)),
                dma((2, 2, PLANE)),
                dma((2, 2, PLANE)),
                dma((2, 2, PLANE)),
                dma((2, NX)),
                dma((2, NX)),
                dma((2, 2, PLANE)),
                dma((2, 2, PLANE)),
                dma((2, blocks)),
                dma((2, blocks)),
                dma,
                dma,
                dma,
                dma,
            ],
            compiler_params=pltpu.CompilerParams(
                collective_id=0, has_side_effects=True, vmem_limit_bytes=56 << 20
            ),
        )(queries, out_grad, prompt_keys, prompt_values, resp_prompt, resp_len)
        grads = [pltpu.with_memory_space_constraint(grad, pltpu.VMEM) for grad in grads]
        return pl.pallas_call(
            store_kernel,
            out_shape=tuple(pltpu.HBM(grad.shape, BF16) for grad in grads),
            in_specs=[in_vmem] * 3,
            out_specs=(pl.BlockSpec(memory_space=pltpu.HBM),) * 3,
            scratch_shapes=[dma((3,))],
        )(*grads)

    rows = P(("blk", "resp"), "head")
    blocks_in = P(None, "blk", "head")
    each = P(("blk", "resp"))
    sums = P(None, ("blk", "resp"), "head")
    return jax.shard_map(
        shards,
        mesh=mesh,
        in_specs=(rows, rows, blocks_in, blocks_in, each, each),
        out_specs=(rows, sums, sums),
        check_vma=False,
    )
```
